128 devices in a mesh: row: 16 (over x, z_hi, core), col: 8 (over z_lo, y).
Axes of the slice: x: 4, y: 4, z: 4 (z_hi: 2, z_lo: 2; z = z_hi * 2 + z_lo), core: 2. Of those that a mesh axis runs over, the one named last changes fastest.
Arguments:
- hidden_acts: bfloat16 [1, 512, 28672], P(None, 'col', 'row'), may hold values from -6 to 6
- out_grads: bfloat16 [1, 512, 8192], P(None, 'row', 'col'), may hold values from -0.119628906 to 0.119628906
- second_moment: float32 [28672, 8192], P('row', 'col'), may hold values from 0.01 to 1
- sign_flips: bfloat16 [28672, 8192], P('row', 'col'), may hold values from -1 to 1, as said below
- kept_rows: int32 [1, 16384], replicated, may hold values from 0 to 32767
- kept_cols: int32 [1, 16384], replicated, may hold values from 0 to 8191
Outputs:
- sketch: float32 [1, 16384], P(None, ('row', 'col'))
The draws below stay inside these ranges and needn't reach their ends.
Inputs may be any that keep to these rules, and one draw needn't show every extreme that they name: `sign_flips`: every entry is +1 or -1.
All inputs are finite; a program needn't handle non-finite values.
Results may differ from the reference program's by a relative error of at most 0.0003.
Values may be sent and summed in bfloat16 or wider, within the bound.
No kernel may reach another device: no remote copies, remote signals or barrier semaphores. Data moves between devices by JAX's collectives and lax.ppermute only.
A program may use at most 128 MiB of HBM per device.

```python
import math
import jax
import jax.numpy as jnp
from jax import lax

D = 8192
FF = 28672
EXAMPLES = 1
TOK = 512
KEEP = 16384
GROUP = 1792
GROUP_PAD = 2048
ROWS_PAD = 32768


def draw_sign_flips(key, part):
    key = jax.random.fold_in(key, 7)
    flips = jax.random.bernoulli(key, 0.5, (FF, D))
    return jnp.where(flips, 1.0, -1.0).astype(jnp.float32).astype(jnp.bfloat16)


def plant(entries, own_key, low, high):
    longest = entries.shape.index(max(entries.shape))
    spots = []
    for shift in (0, 1):
        where = [jax.random.randint(jax.random.fold_in(own_key, axis), (), 0, length) for axis, length in enumerate(entries.shape)]
        where[longest] = (where[longest] + shift) % entries.shape[longest]
        spots.append(tuple(where))
    return entries.at[spots[0]].set(low).at[spots[1]].set(high)


def shard_levels(stream_key, shape, cuts, least, high):
    def one(dim, parts):
        heights = jax.random.uniform(jax.random.fold_in(jax.random.fold_in(stream_key, 6), dim), (parts,), jnp.float32, least / len(cuts), high / len(cuts))
        return jnp.repeat(jnp.exp(heights), shape[dim] // parts).reshape((-1,) + (1,) * (len(shape) - dim - 1))

    factor_of = one(*cuts[0])
    for cut in cuts[1:]:
        factor_of = factor_of * one(*cut)
    return factor_of


def gaussian(key, shape, width, limit, shards=(), kind=jnp.bfloat16):
    gain = shard_levels(key, shape, shards, -0.22, 0.18) if shards else 1.0
    entries = jax.random.normal(key, shape, jnp.float32) * width * gain
    return jnp.minimum(jnp.maximum(entries, -limit), limit).astype(kind)


def setup_inputs(seed: int = 0) -> dict:
    arg_keys = jax.random.split(jax.random.key(seed), 7)
    hidden_acts = gaussian(arg_keys[0], (EXAMPLES, TOK, FF), 1.0, 6.0, ((1, 8), (2, 16)))
    out_grads = gaussian(arg_keys[1], (EXAMPLES, TOK, D), 0.02, 0.119628906, ((1, 16), (2, 8)))
    second_moment = jnp.clip(jnp.exp(math.log(1.0) - 4.6051702 * jax.random.uniform(arg_keys[2], (FF, D), jnp.float32) ** shard_levels(arg_keys[2], (FF, D), ((0, 16), (1, 8)), -0.2, 0.2)), 0.01, 1.0)
    sign_flips = draw_sign_flips(jax.random.fold_in(arg_keys[6], 71), 0)
    kept_rows = plant(jax.random.randint(arg_keys[4], (EXAMPLES, KEEP), 0, ROWS_PAD), jax.random.fold_in(arg_keys[4], 1), 0, ROWS_PAD - 1).astype(jnp.int32)
    kept_cols = plant(jax.random.randint(arg_keys[5], (EXAMPLES, KEEP), 0, D), jax.random.fold_in(arg_keys[5], 1), 0, D - 1).astype(jnp.int32)
    return {"hidden_acts": hidden_acts, "out_grads": out_grads, "second_moment": second_moment, "sign_flips": sign_flips, "kept_rows": kept_rows, "kept_cols": kept_cols}


EPSILON = 1e-08

def parity(values, bit_count):
    ones_count = jnp.zeros_like(values)
    for bit_number in range(bit_count):
        ones_count = ones_count + (values >> bit_number & 1)
    return ones_count & 1

def sylvester(matrix_order):
    ordinal = jnp.arange(matrix_order, dtype=jnp.int32)
    bits_set = parity(ordinal[:, None] & ordinal[None, :], matrix_order.bit_length())
    return (1 - 2 * bits_set).astype(jnp.float32)

def fast_transform(block):
    rows_n, cols_n = block.shape
    flat = block.reshape(-1)
    for length, after in ((rows_n, cols_n), (cols_n, 1)):
        stride = 1
        while stride < length:
            radix = min(16, length // stride)
            shaped = flat.reshape(-1, radix, stride * after)
            flat = jnp.einsum('ij,ajm->aim', sylvester(radix), shaped, precision=lax.Precision.HIGHEST).reshape(-1)
            stride = stride * radix
    return flat.reshape(rows_n, cols_n)

def reference(hidden_acts, out_grads, second_moment, sign_flips, kept_rows, kept_cols):
    group_total = FF // GROUP
    norm_scale = 1.0 / math.sqrt(ROWS_PAD * D)
    group_bits = group_total.bit_length()

    def per_example(items):
        acts_example, grads_example, rows_example, cols_example = items
        group_ids = rows_example // GROUP_PAD
        within = rows_example % GROUP_PAD
        flat_index = within * D + cols_example

        def add_group(running, group):
            start = (group * GROUP).astype(jnp.int32)
            acts_slice = lax.dynamic_slice_in_dim(acts_example, start, GROUP, 1)
            gradient = jnp.dot(acts_slice.T, grads_example, preferred_element_type=jnp.float32)
            flip_slice = lax.dynamic_slice_in_dim(sign_flips, start, GROUP, 0).astype(jnp.float32)
            moment_slice = lax.dynamic_slice_in_dim(second_moment, start, GROUP, 0)
            factor = flip_slice / (jnp.sqrt(moment_slice) + EPSILON) * norm_scale
            scaled = gradient * factor
            padded = jnp.pad(scaled, ((0, GROUP_PAD - GROUP), (0, 0)))
            transformed = fast_transform(padded)
            picked = transformed.reshape(-1)[flat_index]
            group_sign = (1 - 2 * parity(group_ids & group, group_bits)).astype(jnp.float32)
            return (running + group_sign * picked, None)
        running, _ = lax.scan(add_group, jnp.zeros((KEEP,), jnp.float32), jnp.arange(group_total, dtype=jnp.int32))
        return running
    return lax.map(per_example, (hidden_acts, out_grads, kept_rows, kept_cols))
```

```python
import functools
import math

import jax
import jax.numpy as jnp
from jax import lax
from jax.experimental import pallas as pl
from jax.experimental.pallas import tpu as pltpu
from jax.sharding import PartitionSpec as P

D = 8192
GROUP = 1792
GROUP_PAD = 2048
ROWS_PAD = 32768
EPSILON = 1e-08

LANES = 128
SUBLANES = 8
TILE = 256


def parity(values):
    for shift in (8, 4, 2, 1):
        values = values ^ (values >> shift)
    return values & 1


def sylvester(order):
    i = lax.broadcasted_iota(jnp.int32, (order, order), 0)
    j = lax.broadcasted_iota(jnp.int32, (order, order), 1)
    return (1 - 2 * parity(i & j)).astype(jnp.float32).astype(jnp.bfloat16)


def halves(x):
    high = x.astype(jnp.bfloat16)
    low = (x - high.astype(jnp.float32)).astype(jnp.bfloat16)
    return high, low


def dot(a, b, a_dim=1):
    return lax.dot_general(a, b, (((a_dim,), (0,)), ((), ())), preferred_element_type=jnp.float32)


def butterflies(xs):
    xs = list(xs)
    step = 1
    while step < len(xs):
        for i in range(len(xs)):
            if not i & step:
                u, v = xs[i], xs[i | step]
                xs[i], xs[i | step] = (u, u) if v is None else (u + v, u - v)
        step *= 2
    return xs


def local_kernel(
    acts_ref, grads_ref, factor_ref, place_ref, lane_ref, sign_ref, out_ref, inner, whole, place, place_sem
):
    copy_in = pltpu.make_async_copy(place_ref, place, place_sem)
    copy_in.start()
    hidden, width = inner.shape
    blocks = hidden // TILE
    padded_blocks = GROUP_PAD // TILE
    strips = width // TILE
    matrix = sylvester(TILE)

    @pl.loop(0, blocks)
    def _(block):
        rows = pl.ds(pl.multiple_of(block * TILE, TILE), TILE)
        scaled = dot(acts_ref[:, rows], grads_ref[...], 0) * factor_ref[rows, :]
        parts = []
        for strip in range(strips):
            high, low = halves(scaled[:, strip * TILE : (strip + 1) * TILE])
            parts.append(dot(high, matrix) + dot(low, matrix))
        for strip, part in enumerate(butterflies(parts)):
            high, low = halves(part)
            inner[rows, strip * TILE : (strip + 1) * TILE] = dot(matrix, high) + dot(matrix, low)

    unrolled = 4

    @pl.loop(0, TILE // (unrolled * SUBLANES))
    def _(step):
        for strip in range(width // LANES):
            for piece in range(unrolled):
                start = pl.multiple_of((step * unrolled + piece) * SUBLANES, SUBLANES)
                xs = [None] * padded_blocks
                for block in range(blocks):
                    xs[block] = inner[
                        pl.ds(block * TILE + start, SUBLANES), strip * LANES : (strip + 1) * LANES
                    ]
                for block, x in enumerate(butterflies(xs)):
                    whole[pl.ds((strip * padded_blocks + block) * TILE + start, SUBLANES), :] = x

    copy_in.wait()
    lane_ids = lax.broadcasted_iota(jnp.int32, (SUBLANES, LANES), 1)
    sublane_ids = lax.broadcasted_iota(jnp.int32, (SUBLANES, LANES), 0)

    @pl.loop(0, out_ref.shape[0] // SUBLANES)
    def _(group):
        rows = pl.ds(pl.multiple_of(group * SUBLANES, SUBLANES), SUBLANES)
        lanes = lane_ref[rows, :]
        picked = jnp.zeros((SUBLANES, LANES), jnp.float32)
        for lane in range(LANES):
            held = None
            for sublane in range(SUBLANES):
                row = whole[pl.ds(place[(group * SUBLANES + sublane) * LANES + lane], 1), :]
                row = jnp.broadcast_to(row, (SUBLANES, LANES))
                held = row if held is None else jnp.where(sublane_ids == sublane, row, held)
            picked = jnp.where(lane_ids == lane, jnp.take_along_axis(held, lanes, axis=1), picked)
        out_ref[rows, :] = picked * sign_ref[rows, :]


def local_contributions(acts, grads, factor, place, lane, sign):
    hidden, width = factor.shape
    in_vmem = pl.BlockSpec(memory_space=pltpu.VMEM)
    return pl.pallas_call(
        local_kernel,
        out_shape=jax.ShapeDtypeStruct(sign.shape, jnp.float32),
        in_specs=[in_vmem] * 3 + [pl.BlockSpec(memory_space=pl.ANY)] + [in_vmem] * 2,
        out_specs=in_vmem,
        scratch_shapes=[
            pltpu.VMEM((hidden, width), jnp.float32),
            pltpu.VMEM((width // LANES * GROUP_PAD, LANES), jnp.float32),
            pltpu.SMEM(place.shape, jnp.int32),
            pltpu.SemaphoreType.DMA(()),
        ],
        compiler_params=pltpu.CompilerParams(vmem_limit_bytes=40 * 2**20),
    )(acts, grads, factor, place, lane, sign)


def gather_tokens(x, axis):
    copies = jnp.broadcast_to(x[None], (lax.axis_size(axis),) + x.shape)
    return lax.all_to_all(copies, axis, 0, 0, tiled=True).reshape(-1, x.shape[1])


def shards(hidden_acts, out_grads, second_moment, sign_flips, kept_rows, kept_cols):
    examples = hidden_acts.shape[0]
    devices = lax.axis_size("row") * lax.axis_size("col")
    my_row = lax.axis_index("row")
    my_col = lax.axis_index("col")
    hidden, width = second_moment.shape
    norm_scale = 1.0 / math.sqrt(ROWS_PAD * D)
    factor = sign_flips.astype(jnp.float32) / (jnp.sqrt(second_moment) + EPSILON) * norm_scale
    outs = []
    for example in range(examples):
        acts = gather_tokens(hidden_acts[example], "col")
        grads = gather_tokens(out_grads[example], "row")
        rows = kept_rows[example]
        cols = kept_cols[example]
        offset_col = cols % width
        place = offset_col // LANES * GROUP_PAD + rows % GROUP_PAD
        lane = (offset_col % LANES).reshape(devices, -1)
        flips = parity(rows // GROUP_PAD & my_row) ^ parity(cols // width & my_col)
        sign = (1 - 2 * flips).astype(jnp.float32).reshape(devices, -1)
        contribution = local_contributions(acts, grads, factor, place, lane, sign)
        received = lax.all_to_all(contribution, ("row", "col"), 0, 0, tiled=True)
        outs.append(jnp.sum(received, axis=0))
    return jnp.stack(outs)


def solution(mesh):
    placed = (
        P(None, "col", "row"),
        P(None, "row", "col"),
        P("row", "col"),
        P("row", "col"),
        P(),
        P(),
    )
    return jax.shard_map(
        shards, mesh=mesh, in_specs=placed, out_specs=P(None, ("row", "col")), check_vma=False
    )
```

```python
import functools
import math

import jax
import jax.numpy as jnp
from jax import lax
from jax.experimental import pallas as pl
from jax.experimental.pallas import tpu as pltpu
from jax.sharding import PartitionSpec as P

D = 8192
GROUP = 1792
GROUP_PAD = 2048
ROWS_PAD = 32768
EPSILON = 1e-08
NORM_SCALE = 1.0 / math.sqrt(ROWS_PAD * D)

LANES = 128
SUBLANES = 8
TILE = 256


def parity(values):
    for shift in (8, 4, 2, 1):
        values = values ^ (values >> shift)
    return values & 1


def sylvester(order):
    i = lax.broadcasted_iota(jnp.int32, (order, order), 0)
    j = lax.broadcasted_iota(jnp.int32, (order, order), 1)
    return (1 - 2 * parity(i & j)).astype(jnp.float32).astype(jnp.bfloat16)


def halves(x):
    high = x.astype(jnp.bfloat16)
    low = (x - high.astype(jnp.float32)).astype(jnp.bfloat16)
    return high, low


def dot(a, b, a_dim=1):
    return lax.dot_general(a, b, (((a_dim,), (0,)), ((), ())), preferred_element_type=jnp.float32)


def butterflies(xs):
    xs = list(xs)
    step = 1
    while step < len(xs):
        for i in range(len(xs)):
            if not i & step:
                u, v = xs[i], xs[i | step]
                xs[i], xs[i | step] = (u, u) if v is None else (u + v, u - v)
        step *= 2
    return xs


def local_kernel(masks, acts_ref, moment_ref, flips_ref, place_ref, lane_ref, sign_ref, *rest):
    pieces, rest = rest[: len(masks)], rest[len(masks) :]
    out_ref, grads_ref, moment, flips, inner, whole, place, place_sem, moment_sem, flips_sem = rest
    blocks = inner.shape[0] // TILE
    copies_in = []
    for block in range(blocks):
        rows = pl.ds(block * TILE, TILE)
        for source, target, sem in (
            (moment_ref, moment, moment_sem),
            (flips_ref, flips, flips_sem),
        ):
            copies_in.append(
                pltpu.make_async_copy(source.at[rows, :], target.at[rows, :], sem.at[block])
            )
            copies_in[-1].start()
    copy_in = pltpu.make_async_copy(place_ref, place, place_sem)
    copy_in.start()
    mine = lax.axis_index("row")
    for piece, piece_masks in zip(pieces, masks):
        tokens = piece.shape[1]
        for number, mask in enumerate(piece_masks):
            start = pl.multiple_of((mine ^ mask) * tokens, tokens)
            grads_ref[pl.ds(start, tokens), :] = piece[number]
    width = inner.shape[1]
    padded_blocks = GROUP_PAD // TILE
    strips = width // TILE
    matrix = sylvester(TILE)

    @pl.loop(0, blocks)
    def _(block):
        rows = pl.ds(pl.multiple_of(block * TILE, TILE), TILE)
        for source, target, sem in (
            (moment_ref, moment, moment_sem),
            (flips_ref, flips, flips_sem),
        ):
            pltpu.make_async_copy(source.at[rows, :], target.at[rows, :], sem.at[block]).wait()
        factor = flips[rows, :].astype(jnp.float32) / (jnp.sqrt(moment[rows, :]) + EPSILON)
        scaled = dot(acts_ref[:, rows], grads_ref[...], 0) * (factor * NORM_SCALE)
        parts = []
        for strip in range(strips):
            high, low = halves(scaled[:, strip * TILE : (strip + 1) * TILE])
            parts.append(dot(high, matrix) + dot(low, matrix))
        for strip, part in enumerate(butterflies(parts)):
            high, low = halves(part)
            inner[rows, strip * TILE : (strip + 1) * TILE] = dot(matrix, high) + dot(matrix, low)

    unrolled = 4

    @pl.loop(0, TILE // (unrolled * SUBLANES))
    def _(step):
        for strip in range(width // LANES):
            for piece in range(unrolled):
                start = pl.multiple_of((step * unrolled + piece) * SUBLANES, SUBLANES)
                xs = [None] * padded_blocks
                for block in range(blocks):
                    xs[block] = inner[
                        pl.ds(block * TILE + start, SUBLANES), strip * LANES : (strip + 1) * LANES
                    ]
                for block, x in enumerate(butterflies(xs)):
                    whole[pl.ds((strip * padded_blocks + block) * TILE + start, SUBLANES), :] = x

    copy_in.wait()
    lane_ids = lax.broadcasted_iota(jnp.int32, (SUBLANES, LANES), 1)
    sublane_ids = lax.broadcasted_iota(jnp.int32, (SUBLANES, LANES), 0)

    @pl.loop(0, out_ref.shape[0] // SUBLANES)
    def _(group):
        rows = pl.ds(pl.multiple_of(group * SUBLANES, SUBLANES), SUBLANES)
        lanes = lane_ref[rows, :]
        picked = jnp.zeros((SUBLANES, LANES), jnp.float32)
        for lane in range(LANES):
            held = None
            for sublane in range(SUBLANES):
                row = whole[pl.ds(place[(group * SUBLANES + sublane) * LANES + lane], 1), :]
                row = jnp.broadcast_to(row, (SUBLANES, LANES))
                held = row if held is None else jnp.where(sublane_ids == sublane, row, held)
            picked = jnp.where(lane_ids == lane, jnp.take_along_axis(held, lanes, axis=1), picked)
        out_ref[rows, :] = picked * sign_ref[rows, :]


def local_contributions(acts, grads, moment, flips, place, lane, sign):
    hidden, width = moment.shape
    masks, pieces = zip(*grads)
    acts = acts.reshape(-1, hidden)
    in_vmem = pl.BlockSpec(memory_space=pltpu.VMEM)
    anywhere = pl.BlockSpec(memory_space=pl.ANY)
    return pl.pallas_call(
        functools.partial(local_kernel, masks),
        out_shape=jax.ShapeDtypeStruct(sign.shape, jnp.float32),
        in_specs=[in_vmem] + [anywhere] * 3 + [in_vmem] * (2 + len(pieces)),
        out_specs=in_vmem,
        scratch_shapes=[
            pltpu.VMEM((acts.shape[0], width), jnp.bfloat16),
            pltpu.VMEM((hidden, width), jnp.float32),
            pltpu.VMEM((hidden, width), jnp.bfloat16),
            pltpu.VMEM((hidden, width), jnp.float32),
            pltpu.VMEM((width // LANES * GROUP_PAD, LANES), jnp.float32),
            pltpu.SMEM(place.shape, jnp.int32),
            pltpu.SemaphoreType.DMA(()),
            pltpu.SemaphoreType.DMA((hidden // TILE,)),
            pltpu.SemaphoreType.DMA((hidden // TILE,)),
        ],
        compiler_params=pltpu.CompilerParams(vmem_limit_bytes=48 * 2**20),
    )(acts, moment, flips, place, lane, sign, *pieces)


def swap(x, axis, mask):
    return lax.ppermute(x, axis, [(i, i ^ mask) for i in range(lax.axis_size(axis))])


def gather_acts(x, after):
    peers = lax.axis_size("col")
    copies = jnp.broadcast_to(x[None], (peers,) + x.shape)
    copies, after = lax.optimization_barrier((copies, after))
    return lax.all_to_all(copies, "col", 0, 0, tiled=True)


def gather_grads(pair):
    half = jnp.concatenate([pair] + [swap(pair, "row", mask) for mask in (4, 12, 8)])
    masks = tuple(far ^ near for far in (0, 4, 12, 8) for near in (0, 2))
    other = swap(half, "row", 1)
    return [(masks, half), (tuple(mask ^ 1 for mask in masks), other)]


def shards(hidden_acts, out_grads, second_moment, sign_flips, kept_rows, kept_cols):
    examples = hidden_acts.shape[0]
    devices = lax.axis_size("row") * lax.axis_size("col")
    my_row = lax.axis_index("row")
    my_col = lax.axis_index("col")
    width = second_moment.shape[1]
    outs = []
    for example in range(examples):
        own = out_grads[example][None]
        pair = jnp.concatenate([own, swap(own, "row", 2)])
        acts = gather_acts(hidden_acts[example], pair)
        grads = gather_grads(pair)
        rows = kept_rows[example]
        cols = kept_cols[example]
        offset_col = cols % width
        place = offset_col // LANES * GROUP_PAD + rows % GROUP_PAD
        lane = (offset_col % LANES).reshape(devices, -1)
        flips = parity(rows // GROUP_PAD & my_row) ^ parity(cols // width & my_col)
        sign = (1 - 2 * flips).astype(jnp.float32).reshape(devices, -1)
        contribution = local_contributions(
            acts, grads, second_moment, sign_flips, place, lane, sign
        )
        received = lax.all_to_all(contribution, ("row", "col"), 0, 0, tiled=True)
        outs.append(jnp.sum(received, axis=0))
    return jnp.stack(outs)


def solution(mesh):
    placed = (
        P(None, "col", "row"),
        P(None, "row", "col"),
        P("row", "col"),
        P("row", "col"),
        P(),
        P(),
    )
    return jax.shard_map(
        shards, mesh=mesh, in_specs=placed, out_specs=P(None, ("row", "col")), check_vma=False
    )
```

```python
import functools
import math

import jax
import jax.numpy as jnp
from jax import lax
from jax.experimental import pallas as pl
from jax.experimental.pallas import tpu as pltpu
from jax.sharding import PartitionSpec as P

D = 8192
GROUP = 1792
GROUP_PAD = 2048
ROWS_PAD = 32768
EPSILON = 1e-08
NORM_SCALE = 1.0 / math.sqrt(ROWS_PAD * D)

LANES = 128
SUBLANES = 8
TILE = 256
CHUNK = 64
PLACE_SLOTS = 4


def parity(values):
    for shift in (8, 4, 2, 1):
        values = values ^ (values >> shift)
    return values & 1


def sylvester(order):
    i = lax.broadcasted_iota(jnp.int32, (order, order), 0)
    j = lax.broadcasted_iota(jnp.int32, (order, order), 1)
    return (1 - 2 * parity(i & j)).astype(jnp.float32).astype(jnp.bfloat16)


def halves(x):
    high = x.astype(jnp.bfloat16)
    low = (x - high.astype(jnp.float32)).astype(jnp.bfloat16)
    return high, low


def dot(a, b, a_dim=1):
    return lax.dot_general(a, b, (((a_dim,), (0,)), ((), ())), preferred_element_type=jnp.float32)


def butterflies(xs):
    xs = list(xs)
    step = 1
    while step < len(xs):
        for i in range(len(xs)):
            if not i & step:
                u, v = xs[i], xs[i | step]
                xs[i], xs[i | step] = (u, u) if v is None else (u + v, u - v)
        step *= 2
    return xs


def local_kernel(masks, acts_ref, moment_ref, flips_ref, place_ref, lane_ref, sign_ref, *rest):
    pieces, rest = rest[: len(masks)], rest[len(masks) :]
    out_ref, grads_ref, moment, flips, scaled, half, inner, whole, *rest = rest
    *places, moment_sem, flips_sem, place_sem = rest
    hidden, width = inner.shape
    blocks = hidden // TILE
    padded_blocks = GROUP_PAD // TILE
    strips = width // TILE
    picks = SUBLANES * LANES
    groups = out_ref.shape[0] // SUBLANES

    def block_copies(block):
        rows = pl.ds(pl.multiple_of(block * TILE, TILE), TILE)
        return [
            pltpu.make_async_copy(source.at[rows, :], target.at[rows, :], sem.at[block])
            for source, target, sem in (
                (moment_ref, moment, moment_sem),
                (flips_ref, flips, flips_sem),
            )
        ]

    def place_copy(group, slot):
        return pltpu.make_async_copy(
            place_ref.at[pl.ds(pl.multiple_of(group * picks, picks), picks)],
            places[slot],
            place_sem.at[slot],
        )

    for block in range(blocks):
        for copy in block_copies(block):
            copy.start()
    for slot in range(len(places)):
        place_copy(slot, slot).start()

    mine = lax.axis_index("row")
    for piece, piece_masks in zip(pieces, masks):
        tokens = piece.shape[1]
        for number, mask in enumerate(piece_masks):
            start = pl.multiple_of((mine ^ mask) * tokens, tokens)
            grads_ref[pl.ds(start, tokens), :] = piece[number]

    matrix = sylvester(TILE)
    matrix_beside = jnp.concatenate([matrix, matrix], axis=1)

    def scale(block):
        rows = pl.ds(pl.multiple_of(block * TILE, TILE), TILE)
        acts = acts_ref[:, rows]
        for strip in range(strips):
            cols = slice(strip * TILE, (strip + 1) * TILE)
            v = moment[rows, cols]
            factor = flips[rows, cols].astype(jnp.float32) / (v * lax.rsqrt(v) + EPSILON)
            scaled[:, cols] = dot(acts, grads_ref[:, cols], 0) * factor

    def transform_cols():
        for part in range(TILE // CHUNK):
            part_rows = slice(part * CHUNK, (part + 1) * CHUNK)
            xs = butterflies(
                [scaled[part_rows, strip * TILE : (strip + 1) * TILE] for strip in range(strips)]
            )
            stacked = jnp.concatenate([y for x in xs for y in halves(x)], axis=0)
            stacked = dot(stacked, matrix)
            for strip in range(strips):
                cols = slice(strip * TILE, (strip + 1) * TILE)
                start = 2 * strip * CHUNK
                x = stacked[start : start + CHUNK] + stacked[start + CHUNK : start + 2 * CHUNK]
                high, low = halves(x)
                half[part_rows, cols] = high
                half[TILE + part * CHUNK : TILE + (part + 1) * CHUNK, cols] = low

    def transform_rows(block):
        rows = pl.ds(pl.multiple_of(block * TILE, TILE), TILE)
        for strip in range(strips):
            cols = slice(strip * TILE, (strip + 1) * TILE)
            inner[rows, cols] = dot(matrix_beside, half[:, cols])

    def wait_for(block):
        for copy in block_copies(block):
            copy.wait()

    wait_for(0)
    scale(0)
    wait_for(1)
    transform_cols()
    scale(1)

    @pl.loop(2, blocks)
    def _(block):
        wait_for(block)
        transform_rows(block - 2)
        transform_cols()
        scale(block)

    transform_rows(blocks - 2)
    transform_cols()
    transform_rows(blocks - 1)

    unrolled = 4

    @pl.loop(0, TILE // (unrolled * SUBLANES))
    def _(step):
        for strip in range(width // LANES):
            for piece in range(unrolled):
                start = pl.multiple_of((step * unrolled + piece) * SUBLANES, SUBLANES)
                xs = [None] * padded_blocks
                for block in range(blocks):
                    xs[block] = inner[
                        pl.ds(block * TILE + start, SUBLANES), strip * LANES : (strip + 1) * LANES
                    ]
                for block, x in enumerate(butterflies(xs)):
                    whole[pl.ds((strip * padded_blocks + block) * TILE + start, SUBLANES), :] = x

    lane_ids = lax.broadcasted_iota(jnp.int32, (SUBLANES, LANES), 1)
    sublane_ids = lax.broadcasted_iota(jnp.int32, (SUBLANES, LANES), 0)

    @pl.loop(0, groups // len(places))
    def _(step):
        for slot, place in enumerate(places):
            group = step * len(places) + slot
            place_copy(group, slot).wait()
            rows = pl.ds(pl.multiple_of(group * SUBLANES, SUBLANES), SUBLANES)
            lanes = lane_ref[rows, :]
            picked = jnp.zeros((SUBLANES, LANES), jnp.float32)
            for lane in range(LANES):
                held = None
                for sublane in range(SUBLANES):
                    row = whole[pl.ds(place[sublane * LANES + lane], 1), :]
                    row = jnp.broadcast_to(row, (SUBLANES, LANES))
                    held = row if held is None else jnp.where(sublane_ids == sublane, row, held)
                picked = jnp.where(lane_ids == lane, jnp.take_along_axis(held, lanes, axis=1), picked)
            out_ref[rows, :] = picked * sign_ref[rows, :]

            @pl.when(group + len(places) < groups)
            def _():
                place_copy(group + len(places), slot).start()


def local_contributions(acts, grads, moment, flips, place, lane, sign):
    hidden, width = moment.shape
    masks, pieces = zip(*grads)
    acts = acts.reshape(-1, hidden)
    in_vmem = pl.BlockSpec(memory_space=pltpu.VMEM)
    anywhere = pl.BlockSpec(memory_space=pl.ANY)
    return pl.pallas_call(
        functools.partial(local_kernel, masks),
        out_shape=jax.ShapeDtypeStruct(sign.shape, jnp.float32),
        in_specs=[in_vmem] + [anywhere] * 3 + [in_vmem] * (2 + len(pieces)),
        out_specs=in_vmem,
        scratch_shapes=[
            pltpu.VMEM((acts.shape[0], width), jnp.bfloat16),
            pltpu.VMEM((hidden, width), jnp.float32),
            pltpu.VMEM((hidden, width), jnp.bfloat16),
            pltpu.VMEM((TILE, width), jnp.float32),
            pltpu.VMEM((2 * TILE, width), jnp.bfloat16),
            pltpu.VMEM((hidden, width), jnp.float32),
            pltpu.VMEM((width // LANES * GROUP_PAD, LANES), jnp.float32),
            *[pltpu.SMEM((SUBLANES * LANES,), jnp.int32)] * PLACE_SLOTS,
            pltpu.SemaphoreType.DMA((hidden // TILE,)),
            pltpu.SemaphoreType.DMA((hidden // TILE,)),
            pltpu.SemaphoreType.DMA((PLACE_SLOTS,)),
        ],
        compiler_params=pltpu.CompilerParams(vmem_limit_bytes=48 * 2**20),
    )(acts, moment, flips, place, lane, sign, *pieces)


def swap(x, axis, mask):
    return lax.ppermute(x, axis, [(i, i ^ mask) for i in range(lax.axis_size(axis))])


def gather_acts(x, after):
    peers = lax.axis_size("col")
    copies = jnp.broadcast_to(x[None], (peers,) + x.shape)
    copies, after = lax.optimization_barrier((copies, after))
    return lax.all_to_all(copies, "col", 0, 0, tiled=True)


def gather_grads(pair):
    half = jnp.concatenate([pair] + [swap(pair, "row", mask) for mask in (4, 12, 8)])
    masks = tuple(far ^ near for far in (0, 4, 12, 8) for near in (0, 2))
    other = swap(half, "row", 1)
    return [(masks, half), (tuple(mask ^ 1 for mask in masks), other)]


def shards(hidden_acts, out_grads, second_moment, sign_flips, kept_rows, kept_cols):
    examples = hidden_acts.shape[0]
    devices = lax.axis_size("row") * lax.axis_size("col")
    my_row = lax.axis_index("row")
    my_col = lax.axis_index("col")
    width = second_moment.shape[1]
    outs = []
    for example in range(examples):
        own = out_grads[example][None]
        pair = jnp.concatenate([own, swap(own, "row", 2)])
        acts = gather_acts(hidden_acts[example], pair)
        grads = gather_grads(pair)
        rows = kept_rows[example]
        cols = kept_cols[example]
        offset_col = cols % width
        place = offset_col // LANES * GROUP_PAD + rows % GROUP_PAD
        lane = (offset_col % LANES).reshape(devices, -1)
        flips = parity(rows // GROUP_PAD & my_row) ^ parity(cols // width & my_col)
        sign = ((1 - 2 * flips).astype(jnp.float32) * NORM_SCALE).reshape(devices, -1)
        contribution = local_contributions(
            acts, grads, second_moment, sign_flips, place, lane, sign
        )
        received = lax.all_to_all(contribution, ("row", "col"), 0, 0, tiled=True)
        outs.append(jnp.sum(received, axis=0))
    return jnp.stack(outs)


def solution(mesh):
    placed = (
        P(None, "col", "row"),
        P(None, "row", "col"),
        P("row", "col"),
        P("row", "col"),
        P(),
        P(),
    )
    return jax.shard_map(
        shards, mesh=mesh, in_specs=placed, out_specs=P(None, ("row", "col")), check_vma=False
    )
```

```python
import functools
import math

import jax
import jax.numpy as jnp
from jax import lax
from jax.experimental import pallas as pl
from jax.experimental.pallas import tpu as pltpu
from jax.sharding import PartitionSpec as P

D = 8192
GROUP = 1792
GROUP_PAD = 2048
ROWS_PAD = 32768
EPSILON = 1e-08
NORM_SCALE = 1.0 / math.sqrt(ROWS_PAD * D)

LANES = 128
SUBLANES = 8
TILE = 256
CHUNK = 64
PLACE_SLOTS = 4


def parity(values):
    for shift in (8, 4, 2, 1):
        values = values ^ (values >> shift)
    return values & 1


def sylvester(order):
    i = lax.broadcasted_iota(jnp.int32, (order, order), 0)
    j = lax.broadcasted_iota(jnp.int32, (order, order), 1)
    return (1 - 2 * parity(i & j)).astype(jnp.float32).astype(jnp.bfloat16)


def halves(x):
    high = x.astype(jnp.bfloat16)
    low = (x - high.astype(jnp.float32)).astype(jnp.bfloat16)
    return high, low


def dot(a, b, a_dim=1):
    return lax.dot_general(a, b, (((a_dim,), (0,)), ((), ())), preferred_element_type=jnp.float32)


def butterflies(xs):
    xs = list(xs)
    step = 1
    while step < len(xs):
        for i in range(len(xs)):
            if not i & step:
                u, v = xs[i], xs[i | step]
                xs[i], xs[i | step] = (u, u) if v is None else (u + v, u - v)
        step *= 2
    return xs


def local_kernel(
    example, acts_masks, grads_masks, own_acts, moment_ref, flips_ref, place_ref, lane_ref, sign_ref, *rest
):
    acts_pieces, rest = rest[: len(acts_masks)], rest[len(acts_masks) :]
    grads_pieces, rest = rest[: len(grads_masks)], rest[len(grads_masks) :]
    out_ref, acts_ref, grads_ref, moment, flips, scaled, half, inner, whole, *rest = rest
    own_sem, *rest = rest
    *places, moment_sem, flips_sem, place_sem = rest
    hidden, width = inner.shape
    blocks = hidden // TILE
    padded_blocks = GROUP_PAD // TILE
    strips = width // TILE
    groups = out_ref.shape[0] // SUBLANES

    def block_copies(block):
        rows = pl.ds(pl.multiple_of(block * TILE, TILE), TILE)
        return [
            pltpu.make_async_copy(source.at[rows, :], target.at[rows, :], sem.at[block])
            for source, target, sem in (
                (moment_ref, moment, moment_sem),
                (flips_ref, flips, flips_sem),
            )
        ]

    def place_copy(group, slot):
        return pltpu.make_async_copy(
            place_ref.at[pl.ds(pl.multiple_of(group * SUBLANES, SUBLANES), SUBLANES), :],
            places[slot],
            place_sem.at[slot],
        )


    own_tokens = own_acts.shape[1]
    own_start = pl.multiple_of(lax.axis_index("col") * own_tokens, own_tokens)
    own_copy = pltpu.make_async_copy(
        own_acts.at[example], acts_ref.at[pl.ds(own_start, own_tokens), :], own_sem
    )
    own_copy.start()
    for block in range(blocks):
        for copy in block_copies(block):
            copy.start()
    for slot in range(len(places)):
        place_copy(slot, slot).start()
    for axis, target, masks, pieces in (
        ("col", acts_ref, acts_masks, acts_pieces),
        ("row", grads_ref, grads_masks, grads_pieces),
    ):
        mine = lax.axis_index(axis)
        for piece, piece_masks in zip(pieces, masks):
            tokens = piece.shape[1]
            for number, mask in enumerate(piece_masks):
                start = pl.multiple_of((mine ^ mask) * tokens, tokens)
                target[pl.ds(start, tokens), :] = piece[number]
    own_copy.wait()

    matrix = sylvester(TILE)
    matrix_beside = jnp.concatenate([matrix, matrix], axis=1)

    def scale(block):
        rows = pl.ds(pl.multiple_of(block * TILE, TILE), TILE)
        acts = acts_ref[:, rows]
        for strip in range(strips):
            cols = slice(strip * TILE, (strip + 1) * TILE)
            v = moment[rows, cols]
            factor = flips[rows, cols].astype(jnp.float32) / (v * lax.rsqrt(v) + EPSILON)
            scaled[:, cols] = dot(acts, grads_ref[:, cols], 0) * factor

    def transform_cols():
        for part in range(TILE // CHUNK):
            part_rows = slice(part * CHUNK, (part + 1) * CHUNK)
            xs = butterflies(
                [scaled[part_rows, strip * TILE : (strip + 1) * TILE] for strip in range(strips)]
            )
            stacked = jnp.concatenate([y for x in xs for y in halves(x)], axis=0)
            stacked = dot(stacked, matrix)
            for strip in range(strips):
                cols = slice(strip * TILE, (strip + 1) * TILE)
                start = 2 * strip * CHUNK
                x = stacked[start : start + CHUNK] + stacked[start + CHUNK : start + 2 * CHUNK]
                high, low = halves(x)
                half[part_rows, cols] = high
                half[TILE + part * CHUNK : TILE + (part + 1) * CHUNK, cols] = low

    def transform_rows(block):
        rows = pl.ds(pl.multiple_of(block * TILE, TILE), TILE)
        for strip in range(strips):
            cols = slice(strip * TILE, (strip + 1) * TILE)
            inner[rows, cols] = dot(matrix_beside, half[:, cols])

    def wait_for(block):
        for copy in block_copies(block):
            copy.wait()

    wait_for(0)
    scale(0)
    wait_for(1)
    transform_cols()
    scale(1)

    @pl.loop(2, blocks)
    def _(block):
        wait_for(block)
        transform_rows(block - 2)
        transform_cols()
        scale(block)

    transform_rows(blocks - 2)
    transform_cols()
    transform_rows(blocks - 1)

    unrolled = 4

    @pl.loop(0, TILE // (unrolled * SUBLANES))
    def _(step):
        for strip in range(width // LANES):
            for piece in range(unrolled):
                start = pl.multiple_of((step * unrolled + piece) * SUBLANES, SUBLANES)
                xs = [None] * padded_blocks
                for block in range(blocks):
                    xs[block] = inner[
                        pl.ds(block * TILE + start, SUBLANES), strip * LANES : (strip + 1) * LANES
                    ]
                for block, x in enumerate(butterflies(xs)):
                    whole[pl.ds((strip * padded_blocks + block) * TILE + start, SUBLANES), :] = x

    lane_ids = lax.broadcasted_iota(jnp.int32, (SUBLANES, LANES), 1)
    sublane_ids = lax.broadcasted_iota(jnp.int32, (SUBLANES, LANES), 0)

    @pl.loop(0, groups // len(places))
    def _(step):
        for slot, place in enumerate(places):
            group = step * len(places) + slot
            place_copy(group, slot).wait()
            rows = pl.ds(pl.multiple_of(group * SUBLANES, SUBLANES), SUBLANES)
            lanes = lane_ref[rows, :]
            picked = jnp.zeros((SUBLANES, LANES), jnp.float32)
            for lane in range(LANES):
                held = None
                for sublane in range(SUBLANES):
                    row = whole[pl.ds(place[sublane, lane], 1), :]
                    row = jnp.broadcast_to(row, (SUBLANES, LANES))
                    held = row if held is None else jnp.where(sublane_ids == sublane, row, held)
                picked = jnp.where(lane_ids == lane, jnp.take_along_axis(held, lanes, axis=1), picked)
            out_ref[rows, :] = picked * sign_ref[rows, :]

            @pl.when(group + len(places) < groups)
            def _():
                place_copy(group + len(places), slot).start()


def local_contributions(example, hidden_acts, acts, grads, moment, flips, place, lane, sign):
    hidden, width = moment.shape
    acts_masks, acts = zip(*acts)
    grads_masks, grads = zip(*grads)
    tokens = hidden_acts.shape[1] + sum(x.shape[0] * x.shape[1] for x in acts)
    in_vmem = pl.BlockSpec(memory_space=pltpu.VMEM)
    in_hbm = pl.BlockSpec(memory_space=pltpu.HBM)
    return pl.pallas_call(
        functools.partial(local_kernel, example, acts_masks, grads_masks),
        out_shape=jax.ShapeDtypeStruct(place.shape, jnp.float32),
        in_specs=[in_hbm] * 3 + [in_vmem] * (3 +  len(acts) + len(grads)),
        out_specs=in_vmem,
        scratch_shapes=[
            pltpu.VMEM((tokens, hidden), jnp.bfloat16),
            pltpu.VMEM((tokens, width), jnp.bfloat16),
            pltpu.VMEM((hidden, width), jnp.float32),
            pltpu.VMEM((hidden, width), jnp.bfloat16),
            pltpu.VMEM((TILE, width), jnp.float32),
            pltpu.VMEM((2 * TILE, width), jnp.bfloat16),
            pltpu.VMEM((hidden, width), jnp.float32),
            pltpu.VMEM((width // LANES * GROUP_PAD, LANES), jnp.float32),
            pltpu.SemaphoreType.DMA(()),
            *[pltpu.SMEM((SUBLANES, LANES), jnp.int32)] * PLACE_SLOTS,
            pltpu.SemaphoreType.DMA((hidden // TILE,)),
            pltpu.SemaphoreType.DMA((hidden // TILE,)),
            pltpu.SemaphoreType.DMA((PLACE_SLOTS,)),
        ],
        compiler_params=pltpu.CompilerParams(vmem_limit_bytes=48 * 2**20),
    )(hidden_acts, moment, flips, place, lane, sign, *acts, *grads)


def swap(x, axis, mask):
    return lax.ppermute(x, axis, [(i, i ^ mask) for i in range(lax.axis_size(axis))])


def gather(acts, grads, meanwhile):
    own = grads[None]
    near = swap(own, "row", 2)
    held = {0: acts[None]}
    for mask in (4, 1, 3):
        held[mask] = swap(held[0], "col", mask)
    far = swap(held[0], "col", 6)
    held, near, meanwhile = lax.optimization_barrier((held, near, meanwhile))
    held[5] = swap(held[4], "col", 1)
    held[2] = swap(held[1], "col", 3)
    held[7] = swap(held[3], "col", 4)
    held[6] = far
    pair = jnp.concatenate([own, near])
    half = jnp.concatenate([pair] + [swap(pair, "row", mask) for mask in (4, 12, 8)])
    held, half = lax.optimization_barrier((held, half))
    other = swap(half, "row", 1)
    acts = [((mask,), piece) for mask, piece in held.items() if mask]
    masks = tuple(far ^ near for far in (0, 4, 12, 8) for near in (0, 2))
    return acts, [(masks, half), (tuple(mask ^ 1 for mask in masks), other)], meanwhile


def shards(hidden_acts, out_grads, second_moment, sign_flips, kept_rows, kept_cols):
    examples = hidden_acts.shape[0]
    devices = lax.axis_size("row") * lax.axis_size("col")
    my_row = lax.axis_index("row")
    my_col = lax.axis_index("col")
    width = second_moment.shape[1]
    outs = []
    for example in range(examples):
        rows = kept_rows[example].reshape(devices, -1)
        cols = kept_cols[example].reshape(devices, -1)
        place = cols % width // LANES * GROUP_PAD + rows % GROUP_PAD
        lane = cols % LANES
        flips = parity(rows // GROUP_PAD & my_row) ^ parity(cols // width & my_col)
        sign = jnp.where(flips == 1, -NORM_SCALE, NORM_SCALE)
        acts, grads, picks = gather(hidden_acts[example], out_grads[example], (place, lane, sign))
        contribution = local_contributions(
            example, hidden_acts, acts, grads, second_moment, sign_flips, *picks
        )
        received = lax.all_to_all(contribution, ("row", "col"), 0, 0, tiled=True)
        outs.append(jnp.sum(received, axis=0))
    return jnp.stack(outs)


def solution(mesh):
    placed = (
        P(None, "col", "row"),
        P(None, "row", "col"),
        P("row", "col"),
        P("row", "col"),
        P(),
        P(),
    )
    return jax.shard_map(
        shards, mesh=mesh, in_specs=placed, out_specs=P(None, ("row", "col")), check_vma=False
    )
```

```python
import functools
import math

import jax
import jax.numpy as jnp
from jax import lax
from jax.experimental import pallas as pl
from jax.experimental.pallas import tpu as pltpu
from jax.sharding import PartitionSpec as P

D = 8192
GROUP = 1792
GROUP_PAD = 2048
ROWS_PAD = 32768
EPSILON = 1e-08
NORM_SCALE = 1.0 / math.sqrt(ROWS_PAD * D)

LANES = 128
SUBLANES = 8
TILE = 256
CHUNK = 64
PLACE_SLOTS = 2
PLACE_ROWS = 32


def parity(values):
    for shift in (8, 4, 2, 1):
        values = values ^ (values >> shift)
    return values & 1


def sylvester(order):
    i = lax.broadcasted_iota(jnp.int32, (order, order), 0)
    j = lax.broadcasted_iota(jnp.int32, (order, order), 1)
    return (1 - 2 * parity(i & j)).astype(jnp.float32).astype(jnp.bfloat16)


def halves(x):
    high = x.astype(jnp.bfloat16)
    low = (x - high.astype(jnp.float32)).astype(jnp.bfloat16)
    return high, low


def dot(a, b, a_dim=1):
    return lax.dot_general(a, b, (((a_dim,), (0,)), ((), ())), preferred_element_type=jnp.float32)


def butterflies(xs):
    xs = list(xs)
    step = 1
    while step < len(xs):
        for i in range(len(xs)):
            if not i & step:
                u, v = xs[i], xs[i | step]
                xs[i], xs[i | step] = (u, u) if v is None else (u + v, u - v)
        step *= 2
    return xs


def local_kernel(
    acts_masks, grads_masks, moment_ref, flips_ref, place_ref, lane_ref, sign_ref, *rest
):
    acts_pieces, rest = rest[: len(acts_masks)], rest[len(acts_masks) :]
    grads_pieces, rest = rest[: len(grads_masks)], rest[len(grads_masks) :]
    out_ref, acts_ref, grads_ref, moment, flips, scaled, half, inner, whole, *rest = rest
    *places, moment_sem, flips_sem, place_sem = rest
    hidden, width = inner.shape
    blocks = hidden // TILE
    padded_blocks = GROUP_PAD // TILE
    strips = width // TILE
    groups = out_ref.shape[0] // PLACE_ROWS

    def block_copies(block):
        rows = pl.ds(pl.multiple_of(block * TILE, TILE), TILE)
        return [
            pltpu.make_async_copy(source.at[rows, :], target.at[rows, :], sem.at[block])
            for source, target, sem in (
                (moment_ref, moment, moment_sem),
                (flips_ref, flips, flips_sem),
            )
        ]

    def place_copy(group, slot):
        return pltpu.make_async_copy(
            place_ref.at[pl.ds(pl.multiple_of(group * PLACE_ROWS, PLACE_ROWS), PLACE_ROWS), :],
            places[slot],
            place_sem.at[slot],
        )

    for block in range(blocks):
        for copy in block_copies(block):
            copy.start()
    for slot in range(len(places)):
        place_copy(slot, slot).start()
    for axis, target, masks, pieces in (
        ("col", acts_ref, acts_masks, acts_pieces),
        ("row", grads_ref, grads_masks, grads_pieces),
    ):
        mine = lax.axis_index(axis)
        for piece, piece_masks in zip(pieces, masks):
            tokens = piece.shape[1]
            for number, mask in enumerate(piece_masks):
                start = pl.multiple_of((mine ^ mask) * tokens, tokens)
                target[pl.ds(start, tokens), :] = piece[number]

    matrix = sylvester(TILE)
    matrix_beside = jnp.concatenate([matrix, matrix], axis=1)

    def scale(block):
        rows = pl.ds(pl.multiple_of(block * TILE, TILE), TILE)
        acts = acts_ref[:, rows]
        for strip in range(strips):
            cols = slice(strip * TILE, (strip + 1) * TILE)
            v = moment[rows, cols]
            factor = flips[rows, cols].astype(jnp.float32) / (v * lax.rsqrt(v) + EPSILON)
            scaled[:, cols] = dot(acts, grads_ref[:, cols], 0) * factor

    def transform_cols():
        for part in range(TILE // CHUNK):
            part_rows = slice(part * CHUNK, (part + 1) * CHUNK)
            xs = butterflies(
                [scaled[part_rows, strip * TILE : (strip + 1) * TILE] for strip in range(strips)]
            )
            stacked = jnp.concatenate([y for x in xs for y in halves(x)], axis=0)
            stacked = dot(stacked, matrix)
            for strip in range(strips):
                cols = slice(strip * TILE, (strip + 1) * TILE)
                start = 2 * strip * CHUNK
                x = stacked[start : start + CHUNK] + stacked[start + CHUNK : start + 2 * CHUNK]
                high, low = halves(x)
                half[part_rows, cols] = high
                half[TILE + part * CHUNK : TILE + (part + 1) * CHUNK, cols] = low

    def transform_rows(block):
        rows = pl.ds(pl.multiple_of(block * TILE, TILE), TILE)
        for strip in range(strips):
            cols = slice(strip * TILE, (strip + 1) * TILE)
            inner[rows, cols] = dot(matrix_beside, half[:, cols])

    def wait_for(block):
        for copy in block_copies(block):
            copy.wait()

    wait_for(0)
    scale(0)
    wait_for(1)
    transform_cols()
    scale(1)

    @pl.loop(2, blocks)
    def _(block):
        wait_for(block)
        transform_rows(block - 2)
        transform_cols()
        scale(block)

    transform_rows(blocks - 2)
    transform_cols()
    transform_rows(blocks - 1)

    unrolled = 4

    @pl.loop(0, TILE // (unrolled * SUBLANES))
    def _(step):
        for strip in range(width // LANES):
            for piece in range(unrolled):
                start = pl.multiple_of((step * unrolled + piece) * SUBLANES, SUBLANES)
                xs = [None] * padded_blocks
                for block in range(blocks):
                    xs[block] = inner[
                        pl.ds(block * TILE + start, SUBLANES), strip * LANES : (strip + 1) * LANES
                    ]
                for block, x in enumerate(butterflies(xs)):
                    whole[pl.ds((strip * padded_blocks + block) * TILE + start, SUBLANES), :] = x

    lane_ids = lax.broadcasted_iota(jnp.int32, (SUBLANES, LANES), 1)
    sublane_ids = lax.broadcasted_iota(jnp.int32, (SUBLANES, LANES), 0)

    @pl.loop(0, groups // len(places))
    def _(step):
        for slot, place in enumerate(places):
            group = step * len(places) + slot
            place_copy(group, slot).wait()
            for part in range(0, PLACE_ROWS, SUBLANES):
                rows = pl.ds(pl.multiple_of(group * PLACE_ROWS + part, SUBLANES), SUBLANES)
                lanes = lane_ref[rows, :]
                picked = jnp.zeros((SUBLANES, LANES), jnp.float32)
                for lane in range(LANES):
                    held = None
                    for sublane in range(SUBLANES):
                        row = whole[pl.ds(place[part + sublane, lane], 1), :]
                        row = jnp.broadcast_to(row, (SUBLANES, LANES))
                        held = row if held is None else jnp.where(sublane_ids == sublane, row, held)
                    held = jnp.take_along_axis(held, lanes, axis=1)
                    picked = jnp.where(lane_ids == lane, held, picked)
                out_ref[rows, :] = picked * sign_ref[rows, :]

            @pl.when(group + len(places) < groups)
            def _():
                place_copy(group + len(places), slot).start()


def local_contributions(acts, grads, moment, flips, place, lane, sign):
    hidden, width = moment.shape
    acts_masks, acts = zip(*acts)
    grads_masks, grads = zip(*grads)
    tokens = sum(len(own) * x.shape[1] for own, x in zip(grads_masks, grads))
    in_vmem = pl.BlockSpec(memory_space=pltpu.VMEM)
    in_hbm = pl.BlockSpec(memory_space=pltpu.HBM)
    return pl.pallas_call(
        functools.partial(local_kernel, acts_masks, grads_masks),
        out_shape=jax.ShapeDtypeStruct(place.shape, jnp.float32),
        in_specs=[in_hbm] * 2 + [in_vmem] * (3 + len(acts) + len(grads)),
        out_specs=in_vmem,
        scratch_shapes=[
            pltpu.VMEM((tokens, hidden), jnp.bfloat16),
            pltpu.VMEM((tokens, width), jnp.bfloat16),
            pltpu.VMEM((hidden, width), jnp.float32),
            pltpu.VMEM((hidden, width), jnp.bfloat16),
            pltpu.VMEM((TILE, width), jnp.float32),
            pltpu.VMEM((2 * TILE, width), jnp.bfloat16),
            pltpu.VMEM((hidden, width), jnp.float32),
            pltpu.VMEM((width // LANES * GROUP_PAD, LANES), jnp.float32),
            *[pltpu.SMEM((PLACE_ROWS, LANES), jnp.int32)] * PLACE_SLOTS,
            pltpu.SemaphoreType.DMA((hidden // TILE,)),
            pltpu.SemaphoreType.DMA((hidden // TILE,)),
            pltpu.SemaphoreType.DMA((PLACE_SLOTS,)),
        ],
        compiler_params=pltpu.CompilerParams(vmem_limit_bytes=48 * 2**20),
    )(moment, flips, place, lane, sign, *acts, *grads)


def swap(x, axis, mask):
    return lax.ppermute(x, axis, [(i, i ^ mask) for i in range(lax.axis_size(axis))])


def gather(acts, grads, meanwhile):
    own = grads[None]
    near = swap(own, "row", 2)
    held = {0: acts[None]}
    for mask in (4, 1, 3):
        held[mask] = swap(held[0], "col", mask)
    far = swap(held[0], "col", 6)
    mine = jnp.pad(held[0], ((0, 1), (0, 0), (0, 0)))
    held, near, mine, meanwhile = lax.optimization_barrier((held, near, mine, meanwhile))
    held[5] = swap(held[4], "col", 1)
    held[2] = swap(held[1], "col", 3)
    held[7] = swap(held[3], "col", 4)
    held[6] = far
    pair = jnp.concatenate([own, near])
    half = jnp.concatenate([pair] + [swap(pair, "row", mask) for mask in (4, 12, 8)])
    held, half = lax.optimization_barrier((held, half))
    other = swap(half, "row", 1)
    acts = [((mask,), piece) for mask, piece in held.items() if mask] + [((0,), mine)]
    masks = tuple(far ^ near for far in (0, 4, 12, 8) for near in (0, 2))
    return acts, [(masks, half), (tuple(mask ^ 1 for mask in masks), other)], meanwhile


def shards(hidden_acts, out_grads, second_moment, sign_flips, kept_rows, kept_cols):
    examples = hidden_acts.shape[0]
    devices = lax.axis_size("row") * lax.axis_size("col")
    my_row = lax.axis_index("row")
    my_col = lax.axis_index("col")
    width = second_moment.shape[1]
    outs = []
    for example in range(examples):
        rows = kept_rows[example].reshape(devices, -1)
        cols = kept_cols[example].reshape(devices, -1)
        place = cols % width // LANES * GROUP_PAD + rows % GROUP_PAD
        lane = cols % LANES
        flips = parity(rows // GROUP_PAD & my_row) ^ parity(cols // width & my_col)
        sign = jnp.where(flips == 1, -NORM_SCALE, NORM_SCALE)
        acts, grads, picks = gather(hidden_acts[example], out_grads[example], (place, lane, sign))
        contribution = local_contributions(acts, grads, second_moment, sign_flips, *picks)
        received = lax.all_to_all(contribution, ("row", "col"), 0, 0, tiled=True)
        outs.append(jnp.sum(received, axis=0))
    return jnp.stack(outs)


def solution(mesh):
    placed = (
        P(None, "col", "row"),
        P(None, "row", "col"),
        P("row", "col"),
        P("row", "col"),
        P(),
        P(),
    )
    return jax.shard_map(
        shards, mesh=mesh, in_specs=placed, out_specs=P(None, ("row", "col")), check_vma=False
    )
```

```python
import functools
import math

import jax
import jax.numpy as jnp
from jax import lax
from jax.experimental import pallas as pl
from jax.experimental.pallas import tpu as pltpu
from jax.sharding import PartitionSpec as P

D = 8192
GROUP = 1792
GROUP_PAD = 2048
ROWS_PAD = 32768
EPSILON = 1e-08
NORM_SCALE = 1.0 / math.sqrt(ROWS_PAD * D)

LANES = 128
SUBLANES = 8
TILE = 256
CHUNK = 64
PLACE_SLOTS = 2
PLACE_ROWS = 32
EARLY_BLOCKS = 2


def parity(values):
    for shift in (8, 4, 2, 1):
        values = values ^ (values >> shift)
    return values & 1


def sylvester(order):
    i = lax.broadcasted_iota(jnp.int32, (order, order), 0)
    j = lax.broadcasted_iota(jnp.int32, (order, order), 1)
    return (1 - 2 * parity(i & j)).astype(jnp.float32).astype(jnp.bfloat16)


def halves(x):
    high = x.astype(jnp.bfloat16)
    low = (x - high.astype(jnp.float32)).astype(jnp.bfloat16)
    return high, low


def dot(a, b, a_dim=1):
    return lax.dot_general(a, b, (((a_dim,), (0,)), ((), ())), preferred_element_type=jnp.float32)


def butterflies(xs):
    xs = list(xs)
    step = 1
    while step < len(xs):
        for i in range(len(xs)):
            if not i & step:
                u, v = xs[i], xs[i | step]
                xs[i], xs[i | step] = (u, u) if v is None else (u + v, u - v)
        step *= 2
    return xs


def scale_factor(v, flips):
    return flips.astype(jnp.float32) / (v * lax.rsqrt(v) + EPSILON)


def local_kernel(
    acts_masks, grads_masks, moment_ref, flips_ref, place_ref, lane_ref, sign_ref, *rest
):
    early_factors, rest = rest[:EARLY_BLOCKS], rest[EARLY_BLOCKS:]
    acts_pieces, rest = rest[: len(acts_masks)], rest[len(acts_masks) :]
    grads_pieces, rest = rest[: len(grads_masks)], rest[len(grads_masks) :]
    out_ref, acts_ref, grads_ref, moment, flips, scaled, half, inner, whole, *rest = rest
    *places, moment_sem, flips_sem, place_sem = rest
    hidden, width = inner.shape
    blocks = hidden // TILE
    padded_blocks = GROUP_PAD // TILE
    strips = width // TILE
    groups = out_ref.shape[0] // PLACE_ROWS

    def block_copies(block):
        rows = pl.ds(pl.multiple_of(block * TILE, TILE), TILE)
        return [
            pltpu.make_async_copy(source.at[rows, :], target.at[rows, :], sem.at[block])
            for source, target, sem in (
                (moment_ref, moment, moment_sem),
                (flips_ref, flips, flips_sem),
            )
        ]

    def place_copy(group, slot):
        return pltpu.make_async_copy(
            place_ref.at[pl.ds(pl.multiple_of(group * PLACE_ROWS, PLACE_ROWS), PLACE_ROWS), :],
            places[slot],
            place_sem.at[slot],
        )

    for block in range(EARLY_BLOCKS, blocks):
        for copy in block_copies(block):
            copy.start()
    for slot in range(len(places)):
        place_copy(slot, slot).start()
    for axis, target, masks, pieces in (
        ("col", acts_ref, acts_masks, acts_pieces),
        ("row", grads_ref, grads_masks, grads_pieces),
    ):
        mine = lax.axis_index(axis)
        for piece, piece_masks in zip(pieces, masks):
            tokens = piece.shape[1]
            for number, mask in enumerate(piece_masks):
                start = pl.multiple_of((mine ^ mask) * tokens, tokens)
                target[pl.ds(start, tokens), :] = piece[number]

    matrix = sylvester(TILE)
    matrix_beside = jnp.concatenate([matrix, matrix], axis=1)

    def scale(block):
        rows = pl.ds(pl.multiple_of(block * TILE, TILE), TILE)
        acts = acts_ref[:, rows]
        for strip in range(strips):
            cols = slice(strip * TILE, (strip + 1) * TILE)
            if isinstance(block, int) and block < EARLY_BLOCKS:
                factor = early_factors[block][:, cols]
            else:
                factor = scale_factor(moment[rows, cols], flips[rows, cols])
            scaled[:, cols] = dot(acts, grads_ref[:, cols], 0) * factor

    def transform_cols():
        for part in range(TILE // CHUNK):
            part_rows = slice(part * CHUNK, (part + 1) * CHUNK)
            xs = butterflies(
                [scaled[part_rows, strip * TILE : (strip + 1) * TILE] for strip in range(strips)]
            )
            stacked = jnp.concatenate([y for x in xs for y in halves(x)], axis=0)
            stacked = dot(stacked, matrix)
            for strip in range(strips):
                cols = slice(strip * TILE, (strip + 1) * TILE)
                start = 2 * strip * CHUNK
                x = stacked[start : start + CHUNK] + stacked[start + CHUNK : start + 2 * CHUNK]
                high, low = halves(x)
                half[part_rows, cols] = high
                half[TILE + part * CHUNK : TILE + (part + 1) * CHUNK, cols] = low

    def transform_rows(block):
        rows = pl.ds(pl.multiple_of(block * TILE, TILE), TILE)
        for strip in range(strips):
            cols = slice(strip * TILE, (strip + 1) * TILE)
            inner[rows, cols] = dot(matrix_beside, half[:, cols])

    def wait_for(block):
        for copy in block_copies(block):
            copy.wait()

    scale(0)
    transform_cols()
    scale(1)

    @pl.loop(2, blocks)
    def _(block):
        wait_for(block)
        transform_rows(block - 2)
        transform_cols()
        scale(block)

    transform_rows(blocks - 2)
    transform_cols()
    transform_rows(blocks - 1)

    unrolled = 4

    @pl.loop(0, TILE // (unrolled * SUBLANES))
    def _(step):
        for strip in range(width // LANES):
            for piece in range(unrolled):
                start = pl.multiple_of((step * unrolled + piece) * SUBLANES, SUBLANES)
                xs = [None] * padded_blocks
                for block in range(blocks):
                    xs[block] = inner[
                        pl.ds(block * TILE + start, SUBLANES), strip * LANES : (strip + 1) * LANES
                    ]
                for block, x in enumerate(butterflies(xs)):
                    whole[pl.ds((strip * padded_blocks + block) * TILE + start, SUBLANES), :] = x

    lane_ids = lax.broadcasted_iota(jnp.int32, (SUBLANES, LANES), 1)
    sublane_ids = lax.broadcasted_iota(jnp.int32, (SUBLANES, LANES), 0)

    @pl.loop(0, groups // len(places))
    def _(step):
        for slot, place in enumerate(places):
            group = step * len(places) + slot
            place_copy(group, slot).wait()
            for part in range(0, PLACE_ROWS, SUBLANES):
                rows = pl.ds(pl.multiple_of(group * PLACE_ROWS + part, SUBLANES), SUBLANES)
                lanes = lane_ref[rows, :]
                picked = jnp.zeros((SUBLANES, LANES), jnp.float32)
                for lane in range(LANES):
                    held = None
                    for sublane in range(SUBLANES):
                        row = whole[pl.ds(place[part + sublane, lane], 1), :]
                        row = jnp.broadcast_to(row, (SUBLANES, LANES))
                        held = row if held is None else jnp.where(sublane_ids == sublane, row, held)
                    held = jnp.take_along_axis(held, lanes, axis=1)
                    picked = jnp.where(lane_ids == lane, held, picked)
                out_ref[rows, :] = picked * sign_ref[rows, :]

            @pl.when(group + len(places) < groups)
            def _():
                place_copy(group + len(places), slot).start()


def local_contributions(acts, grads, moment, flips, early_factors, place, lane, sign):
    hidden, width = moment.shape
    acts_masks, acts = zip(*acts)
    grads_masks, grads = zip(*grads)
    tokens = sum(len(own) * x.shape[1] for own, x in zip(grads_masks, grads))
    in_vmem = pl.BlockSpec(memory_space=pltpu.VMEM)
    in_hbm = pl.BlockSpec(memory_space=pltpu.HBM)
    return pl.pallas_call(
        functools.partial(local_kernel, acts_masks, grads_masks),
        out_shape=jax.ShapeDtypeStruct(place.shape, jnp.float32),
        in_specs=[in_hbm] * 2 + [in_vmem] * (3 + EARLY_BLOCKS + len(acts) + len(grads)),
        out_specs=in_vmem,
        scratch_shapes=[
            pltpu.VMEM((tokens, hidden), jnp.bfloat16),
            pltpu.VMEM((tokens, width), jnp.bfloat16),
            pltpu.VMEM((hidden, width), jnp.float32),
            pltpu.VMEM((hidden, width), jnp.bfloat16),
            pltpu.VMEM((TILE, width), jnp.float32),
            pltpu.VMEM((2 * TILE, width), jnp.bfloat16),
            pltpu.VMEM((hidden, width), jnp.float32),
            pltpu.VMEM((width // LANES * GROUP_PAD, LANES), jnp.float32),
            *[pltpu.SMEM((PLACE_ROWS, LANES), jnp.int32)] * PLACE_SLOTS,
            pltpu.SemaphoreType.DMA((hidden // TILE,)),
            pltpu.SemaphoreType.DMA((hidden // TILE,)),
            pltpu.SemaphoreType.DMA((PLACE_SLOTS,)),
        ],
        compiler_params=pltpu.CompilerParams(vmem_limit_bytes=48 * 2**20),
    )(moment, flips, place, lane, sign, *early_factors, *acts, *grads)


def swap(x, axis, mask):
    return lax.ppermute(x, axis, [(i, i ^ mask) for i in range(lax.axis_size(axis))])


def gather(acts, grads, meanwhile, later):
    own = grads[None]
    near = swap(own, "row", 2)
    held = {0: acts[None]}
    for mask in (4, 1, 3):
        held[mask] = swap(held[0], "col", mask)
    far = swap(held[0], "col", 6)
    mine = jnp.pad(held[0], ((0, 1), (0, 0), (0, 0)))
    held, near, mine, meanwhile = lax.optimization_barrier((held, near, mine, meanwhile))
    held[5] = swap(held[4], "col", 1)
    held[2] = swap(held[1], "col", 3)
    held[7] = swap(held[3], "col", 4)
    held[6] = far
    pair = jnp.concatenate([own, near])
    half = jnp.concatenate([pair] + [swap(pair, "row", mask) for mask in (4, 12, 8)])
    held, half, later = lax.optimization_barrier((held, half, later))
    other = swap(half, "row", 1)
    acts = [((mask,), piece) for mask, piece in held.items() if mask] + [((0,), mine)]
    masks = tuple(far ^ near for far in (0, 4, 12, 8) for near in (0, 2))
    return acts, [(masks, half), (tuple(mask ^ 1 for mask in masks), other)], meanwhile, later


def shards(hidden_acts, out_grads, second_moment, sign_flips, kept_rows, kept_cols):
    examples = hidden_acts.shape[0]
    devices = lax.axis_size("row") * lax.axis_size("col")
    my_row = lax.axis_index("row")
    my_col = lax.axis_index("col")
    width = second_moment.shape[1]
    outs = []
    for example in range(examples):
        rows = kept_rows[example].reshape(devices, -1)
        cols = kept_cols[example].reshape(devices, -1)
        place = cols % width // LANES * GROUP_PAD + rows % GROUP_PAD
        lane = cols % LANES
        flips = parity(rows // GROUP_PAD & my_row) ^ parity(cols // width & my_col)
        sign = jnp.where(flips == 1, -NORM_SCALE, NORM_SCALE)
        early = [
            scale_factor(second_moment[start : start + TILE], sign_flips[start : start + TILE])
            for start in range(0, EARLY_BLOCKS * TILE, TILE)
        ]
        acts, grads, (first, *picks), later = gather(
            hidden_acts[example], out_grads[example], (early[0], place, lane, sign), early[1:]
        )
        contribution = local_contributions(
            acts, grads, second_moment, sign_flips, [first, *later], *picks
        )
        received = lax.all_to_all(contribution, ("row", "col"), 0, 0, tiled=True)
        outs.append(jnp.sum(received, axis=0))
    return jnp.stack(outs)


def solution(mesh):
    placed = (
        P(None, "col", "row"),
        P(None, "row", "col"),
        P("row", "col"),
        P("row", "col"),
        P(),
        P(),
    )
    return jax.shard_map(
        shards, mesh=mesh, in_specs=placed, out_specs=P(None, ("row", "col")), check_vma=False
    )
```

```python
import functools
import math

import jax
import jax.numpy as jnp
from jax import lax
from jax.experimental import pallas as pl
from jax.experimental.pallas import tpu as pltpu
from jax.sharding import PartitionSpec as P

D = 8192
GROUP = 1792
GROUP_PAD = 2048
ROWS_PAD = 32768
EPSILON = 1e-08
NORM_SCALE = 1.0 / math.sqrt(ROWS_PAD * D)

LANES = 128
SUBLANES = 8
TILE = 256
CHUNK = 64
PLACE_SLOTS = 2
PLACE_ROWS = 32
EARLY_BLOCKS = 2


def parity(values):
    for shift in (8, 4, 2, 1):
        values = values ^ (values >> shift)
    return values & 1


def sylvester(order):
    i = lax.broadcasted_iota(jnp.int32, (order, order), 0)
    j = lax.broadcasted_iota(jnp.int32, (order, order), 1)
    return (1 - 2 * parity(i & j)).astype(jnp.float32).astype(jnp.bfloat16)


def halves(x):
    high = x.astype(jnp.bfloat16)
    low = (x - high.astype(jnp.float32)).astype(jnp.bfloat16)
    return high, low


def dot(a, b, a_dim=1):
    return lax.dot_general(a, b, (((a_dim,), (0,)), ((), ())), preferred_element_type=jnp.float32)


def butterflies(xs):
    xs = list(xs)
    step = 1
    while step < len(xs):
        for i in range(len(xs)):
            if not i & step:
                u, v = xs[i], xs[i | step]
                xs[i], xs[i | step] = (u, u) if v is None else (u + v, u - v)
        step *= 2
    return xs


def scale_factor(v, flips):
    return flips.astype(jnp.float32) / (v * lax.rsqrt(v) + EPSILON)


def local_kernel(
    acts_masks, grads_masks, moment_ref, flips_ref, place_ref, lane_ref, sign_ref, *rest
):
    early_factors, rest = rest[:EARLY_BLOCKS], rest[EARLY_BLOCKS:]
    acts_pieces, rest = rest[: len(acts_masks)], rest[len(acts_masks) :]
    grads_pieces, rest = rest[: len(grads_masks)], rest[len(grads_masks) :]
    out_ref, acts_ref, grads_ref, moment, flips, scaled, half, inner, whole, *rest = rest
    *places, moment_sem, flips_sem, place_sem = rest
    hidden, width = inner.shape
    blocks = hidden // TILE
    padded_blocks = GROUP_PAD // TILE
    strips = width // TILE
    groups = out_ref.shape[0] // PLACE_ROWS

    def block_copies(block):
        rows = pl.ds(pl.multiple_of(block * TILE, TILE), TILE)
        return [
            pltpu.make_async_copy(source.at[rows, :], target.at[rows, :], sem.at[block])
            for source, target, sem in (
                (moment_ref, moment, moment_sem),
                (flips_ref, flips, flips_sem),
            )
        ]

    def place_copy(group, slot):
        return pltpu.make_async_copy(
            place_ref.at[pl.ds(pl.multiple_of(group * PLACE_ROWS, PLACE_ROWS), PLACE_ROWS), :],
            places[slot],
            place_sem.at[slot],
        )

    for block in range(EARLY_BLOCKS, EARLY_BLOCKS + 2):
        for copy in block_copies(block):
            copy.start()
    for slot in range(len(places)):
        place_copy(slot, slot).start()
    for axis, target, masks, pieces in (
        ("col", acts_ref, acts_masks, acts_pieces),
        ("row", grads_ref, grads_masks, grads_pieces),
    ):
        mine = lax.axis_index(axis)
        for piece, piece_masks in zip(pieces, masks):
            tokens = piece.shape[1]
            for number, mask in enumerate(piece_masks):
                start = pl.multiple_of((mine ^ mask) * tokens, tokens)
                target[pl.ds(start, tokens), :] = piece[number]

    matrix = sylvester(TILE)
    matrix_beside = jnp.concatenate([matrix, matrix], axis=1)

    def scale(block):
        rows = pl.ds(pl.multiple_of(block * TILE, TILE), TILE)
        acts = acts_ref[:, rows]
        for strip in range(strips):
            cols = slice(strip * TILE, (strip + 1) * TILE)
            if isinstance(block, int) and block < EARLY_BLOCKS:
                factor = early_factors[block][:, cols]
            else:
                factor = scale_factor(moment[rows, cols], flips[rows, cols])
            scaled[:, cols] = dot(acts, grads_ref[:, cols], 0) * factor

    def transform_cols():
        for part in range(TILE // CHUNK):
            part_rows = slice(part * CHUNK, (part + 1) * CHUNK)
            xs = butterflies(
                [scaled[part_rows, strip * TILE : (strip + 1) * TILE] for strip in range(strips)]
            )
            stacked = jnp.concatenate([y for x in xs for y in halves(x)], axis=0)
            stacked = dot(stacked, matrix)
            for strip in range(strips):
                cols = slice(strip * TILE, (strip + 1) * TILE)
                start = 2 * strip * CHUNK
                x = stacked[start : start + CHUNK] + stacked[start + CHUNK : start + 2 * CHUNK]
                high, low = halves(x)
                half[part_rows, cols] = high
                half[TILE + part * CHUNK : TILE + (part + 1) * CHUNK, cols] = low

    def transform_rows(block):
        rows = pl.ds(pl.multiple_of(block * TILE, TILE), TILE)
        for strip in range(strips):
            cols = slice(strip * TILE, (strip + 1) * TILE)
            inner[rows, cols] = dot(matrix_beside, half[:, cols])

    def wait_for(block):
        for copy in block_copies(block):
            copy.wait()

    scale(0)
    for block in range(EARLY_BLOCKS + 2, blocks):
        for copy in block_copies(block):
            copy.start()
    transform_cols()
    scale(1)

    @pl.loop(2, blocks)
    def _(block):
        wait_for(block)
        transform_rows(block - 2)
        transform_cols()
        scale(block)

    transform_rows(blocks - 2)
    transform_cols()
    transform_rows(blocks - 1)

    unrolled = 4

    @pl.loop(0, TILE // (unrolled * SUBLANES))
    def _(step):
        for strip in range(width // LANES):
            for piece in range(unrolled):
                start = pl.multiple_of((step * unrolled + piece) * SUBLANES, SUBLANES)
                xs = [None] * padded_blocks
                for block in range(blocks):
                    xs[block] = inner[
                        pl.ds(block * TILE + start, SUBLANES), strip * LANES : (strip + 1) * LANES
                    ]
                for block, x in enumerate(butterflies(xs)):
                    whole[pl.ds((strip * padded_blocks + block) * TILE + start, SUBLANES), :] = x

    lane_ids = lax.broadcasted_iota(jnp.int32, (SUBLANES, LANES), 1)
    sublane_ids = lax.broadcasted_iota(jnp.int32, (SUBLANES, LANES), 0)

    @pl.loop(0, groups // len(places))
    def _(step):
        for slot, place in enumerate(places):
            group = step * len(places) + slot
            place_copy(group, slot).wait()
            for part in range(0, PLACE_ROWS, SUBLANES):
                rows = pl.ds(pl.multiple_of(group * PLACE_ROWS + part, SUBLANES), SUBLANES)
                lanes = lane_ref[rows, :]
                picked = jnp.zeros((SUBLANES, LANES), jnp.float32)
                for lane in range(LANES):
                    held = None
                    for sublane in range(SUBLANES):
                        row = whole[pl.ds(place[part + sublane, lane], 1), :]
                        row = jnp.broadcast_to(row, (SUBLANES, LANES))
                        held = row if held is None else jnp.where(sublane_ids == sublane, row, held)
                    held = jnp.take_along_axis(held, lanes, axis=1)
                    picked = jnp.where(lane_ids == lane, held, picked)
                out_ref[rows, :] = picked * sign_ref[rows, :]

            @pl.when(group + len(places) < groups)
            def _():
                place_copy(group + len(places), slot).start()


def local_contributions(acts, grads, moment, flips, early_factors, place, lane, sign):
    hidden, width = moment.shape
    acts_masks, acts = zip(*acts)
    grads_masks, grads = zip(*grads)
    tokens = sum(len(own) * x.shape[1] for own, x in zip(grads_masks, grads))
    in_vmem = pl.BlockSpec(memory_space=pltpu.VMEM)
    in_hbm = pl.BlockSpec(memory_space=pltpu.HBM)
    return pl.pallas_call(
        functools.partial(local_kernel, acts_masks, grads_masks),
        out_shape=jax.ShapeDtypeStruct(place.shape, jnp.float32),
        in_specs=[in_hbm] * 2 + [in_vmem] * (3 + EARLY_BLOCKS + len(acts) + len(grads)),
        out_specs=in_vmem,
        scratch_shapes=[
            pltpu.VMEM((tokens, hidden), jnp.bfloat16),
            pltpu.VMEM((tokens, width), jnp.bfloat16),
            pltpu.VMEM((hidden, width), jnp.float32),
            pltpu.VMEM((hidden, width), jnp.bfloat16),
            pltpu.VMEM((TILE, width), jnp.float32),
            pltpu.VMEM((2 * TILE, width), jnp.bfloat16),
            pltpu.VMEM((hidden, width), jnp.float32),
            pltpu.VMEM((width // LANES * GROUP_PAD, LANES), jnp.float32),
            *[pltpu.SMEM((PLACE_ROWS, LANES), jnp.int32)] * PLACE_SLOTS,
            pltpu.SemaphoreType.DMA((hidden // TILE,)),
            pltpu.SemaphoreType.DMA((hidden // TILE,)),
            pltpu.SemaphoreType.DMA((PLACE_SLOTS,)),
        ],
        compiler_params=pltpu.CompilerParams(vmem_limit_bytes=48 * 2**20),
    )(moment, flips, place, lane, sign, *early_factors, *acts, *grads)


def swap(x, axis, mask):
    return lax.ppermute(x, axis, [(i, i ^ mask) for i in range(lax.axis_size(axis))])


def gather(acts, grads, meanwhile, later):
    own = grads[None]
    near = swap(own, "row", 2)
    held = {0: acts[None]}
    for mask in (4, 1, 3):
        held[mask] = swap(held[0], "col", mask)
    far = swap(held[0], "col", 6)
    mine = jnp.pad(held[0], ((0, 1), (0, 0), (0, 0)))
    held, near, mine, meanwhile = lax.optimization_barrier((held, near, mine, meanwhile))
    held[5] = swap(held[4], "col", 1)
    held[2] = swap(held[1], "col", 3)
    held[7] = swap(held[3], "col", 4)
    held[6] = far
    pair = jnp.concatenate([own, near])
    half = jnp.concatenate([pair] + [swap(pair, "row", mask) for mask in (4, 12, 8)])
    held, half, later = lax.optimization_barrier((held, half, later))
    other = swap(half, "row", 1)
    acts = [((mask,), piece) for mask, piece in held.items() if mask] + [((0,), mine)]
    masks = tuple(far ^ near for far in (0, 4, 12, 8) for near in (0, 2))
    return acts, [(masks, half), (tuple(mask ^ 1 for mask in masks), other)], meanwhile, later


def shards(hidden_acts, out_grads, second_moment, sign_flips, kept_rows, kept_cols):
    examples = hidden_acts.shape[0]
    devices = lax.axis_size("row") * lax.axis_size("col")
    my_row = lax.axis_index("row")
    my_col = lax.axis_index("col")
    width = second_moment.shape[1]
    outs = []
    for example in range(examples):
        rows = kept_rows[example].reshape(devices, -1)
        cols = kept_cols[example].reshape(devices, -1)
        place = cols % width // LANES * GROUP_PAD + rows % GROUP_PAD
        lane = cols % LANES
        flips = parity(rows // GROUP_PAD & my_row) ^ parity(cols // width & my_col)
        sign = jnp.where(flips == 1, -NORM_SCALE, NORM_SCALE)
        early = [
            scale_factor(second_moment[start : start + TILE], sign_flips[start : start + TILE])
            for start in range(0, EARLY_BLOCKS * TILE, TILE)
        ]
        acts, grads, (first, *picks), later = gather(
            hidden_acts[example], out_grads[example], (early[0], place, lane, sign), early[1:]
        )
        contribution = local_contributions(
            acts, grads, second_moment, sign_flips, [first, *later], *picks
        )
        received = lax.all_to_all(contribution, ("row", "col"), 0, 0, tiled=True)
        outs.append(jnp.sum(received, axis=0))
    return jnp.stack(outs)


def solution(mesh):
    placed = (
        P(None, "col", "row"),
        P(None, "row", "col"),
        P("row", "col"),
        P("row", "col"),
        P(),
        P(),
    )
    return jax.shard_map(
        shards, mesh=mesh, in_specs=placed, out_specs=P(None, ("row", "col")), check_vma=False
    )
```
